512 devices in a mesh: group: 16 (over y, core), owner: 32 (over z, x).
Axes of the slice: x: 4, y: 8, z: 8, core: 2. Of those that a mesh axis runs over, the one named last changes fastest.
Arguments:
- prefix_store: float32 [1024, 16, 128, 128], P(('group', 'owner')), may hold values from -18 to 18
- queries: bfloat16 [65536, 1024], P(('group', 'owner')), may hold values from -6 to 6
- key_rows: bfloat16 [65536, 1024], P(('group', 'owner')), may hold values from -6 to 6
- values: bfloat16 [65536, 2048], P(('group', 'owner')), may hold values from -6 to 6
- log_decay: float32 [65536, 16], P(('group', 'owner')), may hold values from -1 to 0
- write_rate: float32 [65536, 16], P(('group', 'owner')), may hold values from 0.1 to 1
- hit_state: int32 [512], replicated, may hold values from 0 to 1023
- save_slot: int32 [512], replicated, may hold values from 0 to 511, each once
Outputs:
- head_output: bfloat16 [65536, 2048], P(('group', 'owner'))
- checkpoints: float32 [512, 16, 128, 128], P(('group', 'owner'))
The draws below stay inside these ranges and needn't reach their ends.
Inputs may be any that keep to these rules, and one draw needn't show every extreme that they name: `hit_state`: some stored states are hit by many requests, others by none. `save_slot`: every checkpoint slot is named by exactly one request.
All inputs are finite; a program needn't handle non-finite values.
Results may differ from the reference program's by a relative error of at most 0.001.
Values sent between devices are 32-bit elements; how exact they have to be, the bound alone decides.
A program may use at most 64 MiB of HBM per device.

```python
import math
import jax
import jax.numpy as jnp
import numpy as np
from jax import lax

HV = 16
HK = 8
DK = 128
DV = 128
SUFFIX_TOKENS = 128
SPAN = 64
REQUESTS = 512
TOKENS = 65536
STATES = 1024


def draw_log_decay(key, part):
    key = jax.random.fold_in(key, 11)
    random_subkeys = jax.random.split(key, 7)
    request_batch = TOKENS // SUFFIX_TOKENS
    slow_share = 5
    slow_heads = jax.random.randint(random_subkeys[0], (request_batch, HV), 0, 10) < slow_share
    slow_rate = math.log(10.0) / SUFFIX_TOKENS * jnp.exp(jax.random.uniform(random_subkeys[1], (request_batch, HV), jnp.float32, math.log(0.05), math.log(0.3)))
    fast_rate = math.log(10.0) / jax.random.uniform(random_subkeys[2], (request_batch, HV), jnp.float32, 30.0, 50.0)
    device_factor = jnp.exp(jax.random.uniform(random_subkeys[3], (request_batch, 1), jnp.float32, math.log(0.5), math.log(2.0)))
    baseline_rate = jnp.where(slow_heads, slow_rate, fast_rate) * device_factor
    jaggedness = jax.random.uniform(random_subkeys[4], (request_batch, SUFFIX_TOKENS, HV), jnp.float32, 0.5, 1.5)
    spike_position = jax.random.randint(random_subkeys[5], (request_batch, 3), 0, SUFFIX_TOKENS)
    spike_mask = jnp.any(spike_position[:, :, None] == jnp.arange(SUFFIX_TOKENS)[None, None, :], axis=1).astype(jnp.float32)
    spike_decay_loss = jax.random.uniform(random_subkeys[6], (request_batch, SUFFIX_TOKENS, 1), jnp.float32, 0.2, 0.5)
    spike_rate = -jnp.log(1.0 - spike_decay_loss) * spike_mask[:, :, None]
    combined_rate = baseline_rate[:, None, :] * jaggedness + spike_rate
    return (-combined_rate).reshape(TOKENS, HV).astype(jnp.float32)


def plant(result, key, low, largest):
    spot = [jax.random.randint(jax.random.fold_in(key, axis), (), 0, length) for axis, length in enumerate(result.shape)]
    widest = result.shape.index(max(result.shape))
    neighbour = spot[:widest] + [(spot[widest] + 1) % result.shape[widest]] + spot[widest + 1:]
    return result.at[tuple(spot)].set(low).at[tuple(neighbour)].set(largest)


def levels(stream_key, dims, cuts, least, top_value):
    loudness = 1.0
    for axis_at, parts in cuts:
        draws = jax.random.uniform(jax.random.fold_in(jax.random.fold_in(stream_key, 6), axis_at), (parts,), jnp.float32, least / len(cuts), top_value / len(cuts))
        loudness = loudness * jnp.repeat(jnp.exp(draws), dims[axis_at] // parts).reshape((-1,) + (1,) * (len(dims) - 1 - axis_at))
    return loudness


def cumulative_ranks(amount, slope):
    loads = [(1 << 20) // math.isqrt(standing ** slope) + 1 for standing in range(1, amount + 1)]
    width = 1 + sum(loads) // (1 << 30)
    return np.cumsum(np.array([max(1, weight // width) for weight in loads]))


def skewed_ids(rng, extent, count, skew):
    grid = cumulative_ranks(count, skew)
    ticket = jax.random.randint(jax.random.fold_in(rng, 1), extent, 0, int(grid[count - 1]))
    grade = jnp.searchsorted(jnp.asarray(grid, jnp.int32), ticket, side="right")
    return jax.random.permutation(jax.random.fold_in(rng, 2), count)[grade].astype(jnp.int32)


def bell_draw(key, dims, scale, bound, pieces=(), kind=jnp.bfloat16):
    result = jax.random.normal(key, dims, jnp.float32) * scale
    if len(pieces) > 0:
        result = levels(key, dims, pieces, -0.22, 0.18) * result
    return jnp.clip(result, min=-bound, max=bound).astype(kind)


def setup_inputs(seed: int = 0) -> dict:
    seeds = jax.random.split(jax.random.key(seed), 9)
    prefix_store = bell_draw(seeds[0], (STATES, HV, DK, DV), 3.0, 18.0, ((0, 512),), jnp.float32)
    queries = bell_draw(seeds[1], (TOKENS, HK * DK), 1.0, 6.0, ((0, 512),))
    key_rows = bell_draw(seeds[2], (TOKENS, HK * DK), 1.0, 6.0, ((0, 512),))
    values = bell_draw(seeds[3], (TOKENS, HV * DV), 1.0, 6.0, ((0, 512),))
    log_decay = draw_log_decay(jax.random.fold_in(seeds[8], 71), 0)
    write_rate = jnp.clip(0.1 + 0.9 * jax.random.uniform(seeds[5], (TOKENS, HV), jnp.float32) ** levels(seeds[5], (TOKENS, HV), ((0, 512),), -0.2, 0.2), 0.1, 1.0)
    hit_state = plant(skewed_ids(seeds[6], (REQUESTS,), STATES, 2), jax.random.fold_in(seeds[6], 3), 0, STATES - 1).astype(jnp.int32)
    save_slot = jax.random.permutation(seeds[7], REQUESTS).astype(jnp.int32)
    return dict(prefix_store=prefix_store, queries=queries, key_rows=key_rows, values=values, log_decay=log_decay, write_rate=write_rate, hit_state=hit_state, save_slot=save_slot)


def unit_rows(matrix, head_count, key_dim):
    rows = matrix.astype(jnp.float32).reshape(matrix.shape[0], head_count, key_dim)
    return rows * lax.rsqrt(lax.optimization_barrier(jnp.sum(rows * rows, axis=-1, keepdims=True)) + 1e-06)

def run_blocks(memory, query_hat, key_hat, value_rows, decay_rows, rate_rows, block):
    highest = lax.Precision.HIGHEST
    length = query_hat.shape[0]
    position = jnp.arange(block)
    on_lower = position[:, None] >= position[None, :]
    on_strict = position[:, None] > position[None, :]
    identity = jnp.eye(block, dtype=jnp.float32)
    results = []
    for block_idx in range(length // block):
        first = block_idx * block
        query_blk = query_hat[first:first + block]
        key_blk = key_hat[first:first + block]
        value_blk = value_rows[first:first + block]
        rate_blk = rate_rows[first:first + block].T
        cum_log = jnp.cumsum(decay_rows[first:first + block], axis=0)
        cum_head = cum_log.T
        gap_log = cum_head[:, :, None] - cum_head[:, None, :]
        decay_in = jnp.where(on_lower, jnp.exp(jnp.where(on_lower, gap_log, 0.0)), 0.0)
        key_gram = jnp.einsum('ihd,jhd->hij', key_blk, key_blk, precision=highest)
        amatrix = rate_blk[:, :, None] * key_gram * jnp.where(on_strict, decay_in, 0.0)
        lower_mat = identity[None] + amatrix
        right_mat = identity[None] * rate_blk[:, :, None]
        inverse_t = lax.linalg.triangular_solve(lower_mat, right_mat, left_side=True, lower=True)
        w_keys = jnp.einsum('hij,jhd->hid', inverse_t, key_blk * jnp.exp(cum_log)[:, :, None], precision=highest)
        u_values = jnp.einsum('hij,jhe->hie', inverse_t, value_blk, precision=highest)
        new_values = u_values - jnp.einsum('hid,hde->hie', w_keys, memory, precision=highest)
        scores = jnp.einsum('ihd,jhd->hij', query_blk, key_blk, precision=highest) * decay_in
        block_out = jnp.einsum('ihd,hde->ihe', query_blk * jnp.exp(cum_log)[:, :, None], memory, precision=highest)
        block_out = block_out + jnp.einsum('hij,hje->ihe', scores, new_values, precision=highest)
        tail_decay = jnp.exp(cum_log[-1])
        weighted_keys = key_blk * jnp.exp(cum_log[-1][None, :] - cum_log)[:, :, None]
        memory = tail_decay[:, None, None] * memory + jnp.einsum('ihd,hie->hde', weighted_keys, new_values, precision=highest)
        results.append(block_out)
    return (memory, jnp.concatenate(results, axis=0))

def reference(prefix_store, queries, key_rows, values, log_decay, write_rate, hit_state, save_slot):
    repeats = HV // HK
    query_hat = unit_rows(queries, HK, DK) * DK ** (-0.5)
    key_hat = unit_rows(key_rows, HK, DK)
    query_hat = jnp.repeat(query_hat, repeats, axis=1).reshape(REQUESTS, SUFFIX_TOKENS, HV, DK)
    key_hat = jnp.repeat(key_hat, repeats, axis=1).reshape(REQUESTS, SUFFIX_TOKENS, HV, DK)
    value_rows = values.astype(jnp.float32).reshape(REQUESTS, SUFFIX_TOKENS, HV, DV)
    decay_rows = log_decay.reshape(REQUESTS, SUFFIX_TOKENS, HV)
    rate_rows = write_rate.reshape(REQUESTS, SUFFIX_TOKENS, HV)

    def one_request(inputs):
        query_one, key_one, value_one, decay_one, rate_one, hit_one = inputs
        start = prefix_store[hit_one]
        return run_blocks(start, query_one, key_one, value_one, decay_one, rate_one, SPAN)
    finals, outputs = lax.map(one_request, (query_hat, key_hat, value_rows, decay_rows, rate_rows, hit_state))
    checkpoints = jnp.zeros_like(finals).at[save_slot].set(finals)
    head_output = outputs.reshape(TOKENS, HV * DV).astype(jnp.bfloat16)
    return (head_output, checkpoints)
```

```python
import functools

import jax
import jax.numpy as jnp
from jax import lax
from jax.experimental import pallas as pl
from jax.experimental.pallas import tpu as pltpu
from jax.sharding import PartitionSpec as P

SPAN = 64
F32 = jnp.float32
BF16 = jnp.bfloat16


def split(x):
    hi = x.astype(BF16)
    return hi, (x - hi.astype(F32)).astype(BF16)


def wide(x):
    return jnp.concatenate(split(x), axis=1)


def fold(x):
    half = x.shape[1] // 2
    return x[:, :half] + x[:, half:]


def dot(a, b):
    return lax.dot_general(a, b, (((1,), (0,)), ((), ())), preferred_element_type=F32)


def dot_exact(a, b):
    return fold(dot(a, wide(b)))


def dot_pair(a_wide, b):
    both = wide(b)
    return fold(dot(a_wide, jnp.concatenate([both, both], axis=0)))


def dot_full(a, b):
    return dot_pair(wide(a), b)


def iota(shape, dim):
    return lax.broadcasted_iota(jnp.int32, shape, dim)


def pick(mask, x, axis):
    return jnp.sum(jnp.where(mask, x, jnp.zeros_like(x)), axis=axis, keepdims=True)


class Plan:
    def __init__(self, first, second, n_first, n_second):
        self.axes = (first, second)
        self.sizes = (n_first, n_second)


def kernel(
    groups, owners, chunks, heads, key_heads, length,
    store, q, k, v, ld, wr, hit, slot,
    out, ckpt,
    r1, t1, r2, w3, r3, t3, r4, fin, r5, t5, r6, w7, r7, t7,
    m1, m2, inv, sco, cum_ref, cumt_ref,
    send_sem, recv_sem, own_sem,
):
    total = groups * owners
    me = {"group": lax.axis_index("group"), "owner": lax.axis_index("owner")}
    count = {"group": groups, "owner": owners}
    per_chunk = heads // chunks
    repeat = heads // key_heads

    def route(chunk):
        return ("group", "owner") if chunk % 2 == 0 else ("owner", "group")

    def turn(axis, step):
        odd = step % 2
        n = count[axis]
        offset = (1 - odd) * (step // 2 + 1) + odd * (n - (step + 1) // 2)
        return (me[axis] + offset) % n

    barrier = pltpu.get_barrier_semaphore()
    for axis in ("group", "owner"):
        def greet(step, carry, axis=axis):
            pl.semaphore_signal(
                barrier, inc=1, device_id={axis: turn(axis, step)},
                device_id_type=pl.DeviceIdType.MESH,
            )
            return carry
        lax.fori_loop(0, count[axis] - 1, greet, 0)
    pl.semaphore_wait(barrier, groups + owners - 2)

    def remote(axis, src, dst, chunk, stage, target):
        return pltpu.make_async_remote_copy(
            src_ref=src, dst_ref=dst,
            send_sem=send_sem.at[chunk, stage], recv_sem=recv_sem.at[chunk, stage],
            device_id={axis: target}, device_id_type=pl.DeviceIdType.MESH,
        )

    def send(chunk, stage, axis, src, dst, rows):
        def go(step, carry):
            target = turn(axis, step)
            remote(
                axis,
                src.at[chunk, pl.ds(pl.multiple_of(target * rows, 8), rows)],
                dst.at[chunk, pl.ds(pl.multiple_of(me[axis] * rows, 8), rows)],
                chunk, stage, target,
            ).start()
            return carry
        lax.fori_loop(0, count[axis] - 1, go, 0)

    def keep(chunk, axis, src, dst, rows):
        place = pl.ds(pl.multiple_of(me[axis] * rows, 8), rows)
        dst[chunk, place] = src[chunk, place]

    def await_recv(chunk, stage, axis, dst, rows):
        part = dst.at[chunk, pl.ds(0, (count[axis] - 1) * rows)]
        remote(axis, part, part, chunk, stage, turn(axis, 0)).wait_recv()

    def await_send(chunk, stage, axis, src, rows):
        part = src.at[chunk, pl.ds(0, (count[axis] - 1) * rows)]
        remote(axis, part, part, chunk, stage, turn(axis, 0)).wait_send()

    def regroup(chunk, src, dst, n_outer, n_inner):
        for inner in range(n_inner):
            dst[chunk, pl.ds(inner * n_outer, n_outer), :] = src[
                chunk, pl.ds(inner, n_outer, stride=n_inner), :
            ]

    def select(chunk, matrix, src, dst):
        rows = src.shape[1]
        both = wide(src[chunk])
        strip = 128
        for first in range(0, total, strip):
            dst[chunk, pl.ds(first, strip), :] = fold(
                dot(matrix[chunk % 2, pl.ds(first, strip), :], both)
            )

    def stage1(chunk):
        axis, other = route(chunk)
        rows = count[other]

        def go(step, carry):
            target = turn(axis, step)
            for state in range(2):
                remote(
                    axis,
                    store.at[state, chunk, pl.ds(pl.multiple_of(target * rows, 8), rows)],
                    r1.at[chunk, pl.ds(pl.multiple_of((me[axis] * 2 + state) * rows, 8), rows)],
                    chunk, 0, target,
                ).start()
            return carry
        lax.fori_loop(0, count[axis] - 1, go, 0)
        for state in range(2):
            pltpu.make_async_copy(
                store.at[state, chunk, pl.ds(pl.multiple_of(me[axis] * rows, 8), rows)],
                r1.at[chunk, pl.ds(pl.multiple_of((me[axis] * 2 + state) * rows, 8), rows)],
                own_sem.at[chunk, state],
            ).start()

    def stage2(chunk):
        axis, other = route(chunk)
        rows = count[other]
        for state in range(2):
            pltpu.make_async_copy(
                store.at[state, chunk, pl.ds(pl.multiple_of(me[axis] * rows, 8), rows)],
                r1.at[chunk, pl.ds(pl.multiple_of((me[axis] * 2 + state) * rows, 8), rows)],
                own_sem.at[chunk, state],
            ).wait()
        await_recv(chunk, 0, axis, r1, 2 * rows)
        regroup(chunk, r1, t1, 2 * count[axis], rows)
        send(chunk, 1, other, t1, r2, 2 * count[axis])
        keep(chunk, other, t1, r2, 2 * count[axis])

    def stage3(chunk):
        axis, other = route(chunk)
        await_recv(chunk, 1, other, r2, 2 * count[axis])
        select(chunk, m1, r2, w3)
        send(chunk, 2, other, w3, r3, count[axis])
        keep(chunk, other, w3, r3, count[axis])

    def stage4(chunk):
        axis, other = route(chunk)
        await_recv(chunk, 2, other, r3, count[axis])
        regroup(chunk, r3, t3, count[other], count[axis])
        send(chunk, 3, axis, t3, r4, count[other])
        keep(chunk, axis, t3, r4, count[other])

    def stage5(chunk):
        axis, other = route(chunk)
        await_recv(chunk, 3, axis, r4, count[other])
        advance(chunk)
        send(chunk, 4, axis, fin, r5, count[other])
        keep(chunk, axis, fin, r5, count[other])

    def stage6(chunk):
        axis, other = route(chunk)
        await_recv(chunk, 4, axis, r5, count[other])
        regroup(chunk, r5, t5, count[axis], count[other])
        send(chunk, 5, other, t5, r6, count[axis])
        keep(chunk, other, t5, r6, count[axis])

    def stage7(chunk):
        axis, other = route(chunk)
        await_recv(chunk, 5, other, r6, count[axis])
        select(chunk, m2, r6, w7)
        send(chunk, 6, other, w7, r7, count[axis])
        keep(chunk, other, w7, r7, count[axis])

    def stage8(chunk):
        axis, other = route(chunk)
        await_recv(chunk, 6, other, r7, count[axis])
        regroup(chunk, r7, t7, count[other], count[axis])
        send(chunk, 7, axis, t7, ckpt, count[other])
        keep(chunk, axis, t7, ckpt, count[other])

    def stage9(chunk):
        axis, other = route(chunk)
        await_recv(chunk, 7, axis, ckpt, count[other])

    def index_matrices():
        strip = 128
        hit_row, slot_row = hit[...], slot[...]

        def swap(x):
            return (x % groups) * owners + x // groups

        slot_swapped = jnp.zeros((1, total), jnp.int32)
        for first in range(0, total, strip):
            place = pl.ds(first, strip)
            row = iota((strip, total), 0) + first
            lane = iota((strip, total), 1)
            hit_natural = pick(row == lane, hit_row, 1)
            hit_swapped = pick(swap(row) == lane, hit_row, 1)
            slot_natural = pick(row == lane, slot_row, 1)
            slot_swapped = slot_swapped + pick(row == swap(lane), slot_natural, 0)
            state = iota((strip, 2 * total), 1)
            named = ((state // 2) % groups * owners + state // (2 * groups)) * 2 + state % 2
            one = jnp.ones((), F32)
            zero = jnp.zeros((), F32)
            m1[0, place, :] = jnp.where(hit_swapped == named, one, zero).astype(BF16)
            m1[1, place, :] = jnp.where(hit_natural == state, one, zero).astype(BF16)
            m2[1, place, :] = jnp.where(slot_row == row, one, zero).astype(BF16)
        for first in range(0, total, strip):
            row = iota((strip, total), 0) + first
            m2[0, pl.ds(first, strip), :] = jnp.where(
                slot_swapped == swap(row), one, zero
            ).astype(BF16)

    square = (length, length)

    def same(size):
        return iota(square, 0) // size == iota(square, 1) // size

    def cumulate():
        lower = (iota(square, 0) >= iota(square, 1)) & same(SPAN)
        ones = jnp.where(lower, jnp.ones((), F32), jnp.zeros((), F32))
        cum = jnp.dot(
            ones, ld[...], precision=lax.Precision.HIGHEST, preferred_element_type=F32
        )
        cum_ref[...] = cum
        padded = jnp.concatenate([cum, jnp.zeros((length, length - heads), F32)], axis=1)
        cumt_ref[...] = padded.T[:heads]

    def prepare(chunk, carry):
        row, col = iota(square, 0), iota(square, 1)
        eye = row == col
        lower = (row >= col) & same(SPAN)
        strict = (row > col) & same(SPAN)
        unit = jnp.where(eye, jnp.ones((), F32), jnp.zeros((), F32))
        lane = iota((length, heads), 1)
        key_dim = q.shape[1] // key_heads
        amats = []
        for inner in range(per_chunk // repeat):
            key_head = chunk * (per_chunk // repeat) + inner
            place = pl.ds(pl.multiple_of(key_head * key_dim, 128), key_dim)
            key, query = k[:, place], q[:, place]
            trans = (((1,), (1,)), ((), ()))
            gram = lax.dot_general(key, key, trans, preferred_element_type=F32)
            cross = lax.dot_general(query, key, trans, preferred_element_type=F32)
            key_col = lax.rsqrt(pick(eye, gram, 1) + 1e-06)
            key_row = lax.rsqrt(pick(eye, gram, 0) + 1e-06)
            query32 = query.astype(F32)
            query_col = lax.rsqrt(
                jnp.sum(query32 * query32, axis=1, keepdims=True) + 1e-06
            ) * key_dim ** (-0.5)
            gram = gram * key_col * key_row
            cross = cross * query_col * key_row
            for extra in range(repeat):
                head = key_head * repeat + extra
                cum_col = pick(lane == head, cum_ref[...], 1)
                rate_col = pick(lane == head, wr[...], 1)
                gap = cum_col - cumt_ref[pl.ds(head, 1), :]
                decay = jnp.where(lower, jnp.exp(jnp.where(lower, gap, 0.0)), 0.0)
                sco[head] = wide(cross * decay)
                amats.append((head, jnp.where(strict, rate_col * gram * decay, 0.0)))
        results = []
        small = 8
        within = same(small)
        diag = [jnp.where(within, a, 0.0) for _, a in amats]
        xs = [unit - b for b in diag]
        for _ in range(2):
            diag = [dot_full(b, b) for b in diag]
            xs = [x + dot_full(x, b) for x, b in zip(xs, diag)]
        size = small
        while size < SPAN:
            cross_mask = same(2 * size) & ~same(size)
            parts = [jnp.where(cross_mask, a, 0.0) for _, a in amats]
            inner_products = [dot_full(p, x) for p, x in zip(parts, xs)]
            xs = [x - dot_full(x, p) for x, p in zip(xs, inner_products)]
            size *= 2
        for (head, _), x in zip(amats, xs):
            inv[head] = wide(x)
        return carry

    def advance(chunk):
        key_dim = q.shape[1] // key_heads
        value_dim = v.shape[1] // heads
        head_list = [chunk * per_chunk + i for i in range(per_chunk)]
        states = [r4[chunk, pl.ds(i * key_dim, key_dim), :] for i in range(per_chunk)]
        for first in range(0, length, SPAN):
            rows = pl.ds(first, SPAN)
            block = (first, first + SPAN)
            reads, scales = [], []
            for i, head in enumerate(head_list):
                cols = pl.ds(head // repeat * key_dim, key_dim)
                both = jnp.concatenate([k[rows, cols], q[rows, cols]], axis=0)
                reads.append(dot_exact(both, states[i]))
            news = []
            for i, head in enumerate(head_list):
                cols = pl.ds(head // repeat * key_dim, key_dim)
                key32 = k[rows, cols].astype(F32)
                query32 = q[rows, cols].astype(F32)
                key_scale = lax.rsqrt(jnp.sum(key32 * key32, axis=1, keepdims=True) + 1e-06)
                query_scale = lax.rsqrt(
                    jnp.sum(query32 * query32, axis=1, keepdims=True) + 1e-06
                ) * key_dim ** (-0.5)
                cum_col = cum_ref[rows, head : head + 1]
                last = cum_ref[pl.ds(first + SPAN - 1, 1), head : head + 1]
                grown = jnp.exp(cum_col)
                rate = wr[rows, head : head + 1]
                value = v[rows, pl.ds(head * value_dim, value_dim)].astype(F32)
                rest = rate * (value - (grown * key_scale) * reads[i][:SPAN])
                matrix = inv[head, rows, :]
                left = jnp.concatenate(
                    [matrix[:, first : first + SPAN],
                     matrix[:, length + first : length + first + SPAN]], axis=1
                )
                news.append(dot_pair(left, rest))
                scales.append((query_scale * grown, key_scale * jnp.exp(last - cum_col), jnp.exp(last)))
            for i, head in enumerate(head_list):
                cols = pl.ds(head // repeat * key_dim, key_dim)
                query_scale, key_scale, tail = scales[i]
                matrix = sco[head, rows, :]
                left = jnp.concatenate(
                    [matrix[:, first : first + SPAN],
                     matrix[:, length + first : length + first + SPAN]], axis=1
                )
                result = query_scale * reads[i][SPAN:] + dot_pair(left, news[i])
                out[rows, pl.ds(head * value_dim, value_dim)] = result.astype(out.dtype)
                key_t = k[rows, cols].T
                states[i] = tail * states[i] + dot_exact(key_t, key_scale * news[i])
        for i in range(per_chunk):
            fin[chunk, pl.ds(i * key_dim, key_dim), :] = states[i]

    stage1(0)
    stage1(1)
    index_matrices()
    cumulate()
    lax.fori_loop(0, chunks, prepare, 0)
    stage1(2)
    stage1(3)
    ahead, behind = (0, 1), (2, 3)
    lead = [stage2, stage3, stage4, stage5, stage6, stage7, stage8, stage9]
    for step in range(len(lead) + 1):
        if step < len(lead):
            for chunk in ahead:
                lead[step](chunk)
        if step >= 1:
            for chunk in behind:
                lead[step - 1](chunk)
    for chunk in range(chunks):
        axis, other = route(chunk)
        na, nb = count[axis], count[other]
        await_send(chunk, 0, axis, r1, 2 * nb)
        await_send(chunk, 1, other, t1, 2 * na)
        await_send(chunk, 2, other, w3, na)
        await_send(chunk, 3, axis, t3, nb)
        await_send(chunk, 4, axis, fin, nb)
        await_send(chunk, 5, other, t5, na)
        await_send(chunk, 6, other, w7, na)
        await_send(chunk, 7, axis, t7, nb)


def body(prefix_store, queries, key_rows, values, log_decay, write_rate, hit_state, save_slot):
    groups = lax.axis_size("group")
    owners = lax.axis_size("owner")
    slots, heads, key_dim, value_dim = prefix_store.shape
    total = groups * owners
    length = queries.shape[0]
    key_heads = queries.shape[1] // key_dim
    chunks = heads * key_dim // total
    vmem = pl.BlockSpec(memory_space=pltpu.VMEM)
    anywhere = pl.BlockSpec(memory_space=pl.ANY)
    one = pltpu.VMEM((chunks, total, value_dim), F32)
    two = pltpu.VMEM((chunks, 2 * total, value_dim), F32)
    head_output, checkpoints = pl.pallas_call(
        functools.partial(kernel, groups, owners, chunks, heads, key_heads, length),
        out_shape=(
            jax.ShapeDtypeStruct((length, heads * value_dim), BF16),
            jax.ShapeDtypeStruct((chunks, total, value_dim), F32),
        ),
        in_specs=[anywhere] + [vmem] * 7,
        out_specs=(vmem, vmem),
        scratch_shapes=[
            two, two, two, one, one, one, one, one, one, one, one, one, one, one,
            pltpu.VMEM((2, total, 2 * total), BF16),
            pltpu.VMEM((2, total, total), BF16),
            pltpu.VMEM((heads, length, 2 * length), BF16),
            pltpu.VMEM((heads, length, 2 * length), BF16),
            pltpu.VMEM((length, heads), F32),
            pltpu.VMEM((heads, length), F32),
            pltpu.SemaphoreType.DMA((chunks, 8)),
            pltpu.SemaphoreType.DMA((chunks, 8)),
            pltpu.SemaphoreType.DMA((chunks, 2)),
        ],
        compiler_params=pltpu.CompilerParams(
            collective_id=0, has_side_effects=True, vmem_limit_bytes=56 * 1024 * 1024
        ),
        cost_estimate=pl.CostEstimate(
            flops=4 * 10**9, bytes_accessed=6 * 2**20, transcendentals=2**19
        ),
    )(
        prefix_store.reshape(slots, chunks, total, value_dim),
        queries, key_rows, values, log_decay, write_rate,
        hit_state.reshape(1, total), save_slot.reshape(1, total),
    )
    return head_output, checkpoints.reshape(1, heads, key_dim, value_dim)


def solution(mesh):
    split_rows = P(("group", "owner"), None)
    split_states = P(("group", "owner"), None, None, None)
    in_specs = (split_states,) + (split_rows,) * 5 + (P(), P())
    return jax.shard_map(
        body, mesh=mesh, in_specs=in_specs, out_specs=(split_rows, split_states), check_vma=False
    )
```

```python
import functools

import jax
import jax.numpy as jnp
from jax import lax
from jax.experimental import pallas as pl
from jax.experimental.pallas import tpu as pltpu
from jax.sharding import PartitionSpec as P

SPAN = 64
F32 = jnp.float32
BF16 = jnp.bfloat16


def split(x):
    hi = x.astype(BF16)
    return hi, (x - hi.astype(F32)).astype(BF16)


def wide(x):
    return jnp.concatenate(split(x), axis=1)


def fold(x):
    half = x.shape[1] // 2
    return x[:, :half] + x[:, half:]


def dot(a, b):
    return lax.dot_general(a, b, (((1,), (0,)), ((), ())), preferred_element_type=F32)


def dot_exact(a, b):
    return fold(dot(a, wide(b)))


def dot_pair(a_wide, b):
    both = wide(b)
    return fold(dot(a_wide, jnp.concatenate([both, both], axis=0)))


def dot_full(a, b):
    return dot_pair(wide(a), b)


def iota(shape, dim):
    return lax.broadcasted_iota(jnp.int32, shape, dim)


def pick(mask, x, axis):
    return jnp.sum(jnp.where(mask, x, jnp.zeros_like(x)), axis=axis, keepdims=True)


LOW = {"group": 2, "owner": 4}
CELL, PLANE = 11, 48


def kernel(
    packed, groups, owners, chunks, heads, key_heads, length,
    store, q, k, v, ld, wr, hit, slot,
    *refs,
):
    if packed:
        out, ckpt, flag, *refs = refs
        sv, s0, r0, t0, hc, mk, mf, *refs = refs
    else:
        out, ckpt, *refs = refs
    (
        r1, t1, r2, w3, r3, t3, r4, fin, r5, t5, r6, w7, r7, t7,
        m1, m2, inv, sco, cum_ref, cumt_ref, rate_ref,
        send_sem, recv_sem, own_sem,
    ) = refs
    total = groups * owners
    me = {"group": lax.axis_index("group"), "owner": lax.axis_index("owner")}
    count = {"group": groups, "owner": owners}
    per_chunk = heads // chunks
    repeat = heads // key_heads

    def route(chunk):
        return ("group", "owner") if chunk % 2 == 0 else ("owner", "group")

    low = {axis: me[axis] % LOW[axis] for axis in me}
    high = {axis: me[axis] // LOW[axis] for axis in me}
    highs = {axis: count[axis] // LOW[axis] for axis in me}
    cell = LOW["group"] * LOW["owner"]
    place_in_cell = low["owner"] * LOW["group"] + low["group"]

    def shift(step, n):
        odd = step % 2
        return (1 - odd) * (step // 2 + 1) + odd * (n - (step + 1) // 2)

    def turn(axis, step):
        n, part = count[axis], LOW[axis]
        offset = shift(step, n)
        inner = (low[axis] + offset % part) % part
        outer = (high[axis] + offset // part) % (n // part)
        return outer * part + inner

    def turn_high(axis, step):
        return (high[axis] + shift(step, highs[axis])) % highs[axis]

    def cell_target(index):
        return {
            "group": high["group"] * LOW["group"] + index % LOW["group"],
            "owner": high["owner"] * LOW["owner"] + index // LOW["group"],
        }

    if packed:
        for chunk in range(chunks):
            for state in range(2):
                pltpu.make_async_copy(
                    store.at[state, chunk], sv.at[chunk, state], own_sem.at[chunk, state]
                ).start()

    barrier = pltpu.get_barrier_semaphore()
    for axis in ("group", "owner"):
        def greet(step, carry, axis=axis):
            pl.semaphore_signal(
                barrier, inc=1, device_id={axis: turn(axis, step)},
                device_id_type=pl.DeviceIdType.MESH,
            )
            return carry
        lax.fori_loop(0, count[axis] - 1, greet, 0)
    greeted = groups + owners - 2
    if packed:
        def greet_cell(step, carry):
            inner = (low["owner"] + step + 1) % LOW["owner"]
            pl.semaphore_signal(
                barrier, inc=1,
                device_id=cell_target(inner * LOW["group"] + 1 - low["group"]),
                device_id_type=pl.DeviceIdType.MESH,
            )
            return carry
        lax.fori_loop(0, LOW["owner"] - 1, greet_cell, 0)
        greeted = greeted + LOW["owner"] - 1

    def remote(axis, src, dst, chunk, stage, target):
        return pltpu.make_async_remote_copy(
            src_ref=src, dst_ref=dst,
            send_sem=send_sem.at[chunk, stage], recv_sem=recv_sem.at[chunk, stage],
            device_id={axis: target}, device_id_type=pl.DeviceIdType.MESH,
        )

    def send(chunk, stage, axis, src, dst, rows):
        def go(step, carry):
            target = turn(axis, step)
            remote(
                axis,
                src.at[chunk, pl.ds(pl.multiple_of(target * rows, 8), rows)],
                dst.at[chunk, pl.ds(pl.multiple_of(me[axis] * rows, 8), rows)],
                chunk, stage, target,
            ).start()
            return carry
        lax.fori_loop(0, count[axis] - 1, go, 0)

    def keep(chunk, axis, src, dst, rows):
        place = pl.ds(pl.multiple_of(me[axis] * rows, 8), rows)
        dst[chunk, place] = src[chunk, place]

    def await_recv(chunk, stage, axis, dst, rows):
        part = dst.at[chunk, pl.ds(0, (count[axis] - 1) * rows)]
        remote(axis, part, part, chunk, stage, turn(axis, 0)).wait_recv()

    def await_send(chunk, stage, axis, src, rows):
        part = src.at[chunk, pl.ds(0, (count[axis] - 1) * rows)]
        remote(axis, part, part, chunk, stage, turn(axis, 0)).wait_send()

    def regroup(chunk, src, dst, n_outer, n_inner):
        for inner in range(n_inner):
            dst[chunk, pl.ds(inner * n_outer, n_outer), :] = src[
                chunk, pl.ds(inner, n_outer, stride=n_inner), :
            ]

    def select(chunk, matrix, src, dst):
        rows = src.shape[1]
        both = wide(src[chunk])
        strip = 128
        for first in range(0, total, strip):
            dst[chunk, pl.ds(first, strip), :] = fold(
                dot(matrix[chunk % 2, pl.ds(first, strip), :], both)
            )

    def send_high(chunk, stage, axis, src, dst, rows):
        def go(step, carry):
            target = turn_high(axis, step)
            remote(
                axis,
                src.at[chunk, pl.ds(pl.multiple_of(target * rows, 8), rows)],
                dst.at[chunk, pl.ds(pl.multiple_of(high[axis] * rows, 8), rows)],
                chunk, stage, target * LOW[axis] + low[axis],
            ).start()
            return carry
        lax.fori_loop(0, highs[axis] - 1, go, 0)
        mine = pl.ds(pl.multiple_of(high[axis] * rows, 8), rows)
        dst[chunk, mine] = src[chunk, mine]

    def await_high(chunk, stage, axis, dst, rows):
        part = dst.at[chunk, pl.ds(0, (highs[axis] - 1) * rows)]
        copy = remote(axis, part, part, chunk, stage, turn(axis, 0))
        return copy

    def cell_copy(chunk, target):
        rows = 2 * highs["group"] * highs["owner"]
        return pltpu.make_async_remote_copy(
            src_ref=s0.at[chunk, pl.ds(pl.multiple_of(target * rows, 8), rows)],
            dst_ref=r0.at[chunk, pl.ds(pl.multiple_of(place_in_cell * rows, 8), rows)],
            send_sem=send_sem.at[chunk, 8], recv_sem=recv_sem.at[chunk, 8],
            device_id=cell_target(target), device_id_type=pl.DeviceIdType.MESH,
        )

    def await_cell(chunk, ref):
        rows = 2 * highs["group"] * highs["owner"]
        part = ref.at[chunk, pl.ds(0, (cell - 1) * rows)]
        return pltpu.make_async_remote_copy(
            src_ref=part, dst_ref=part,
            send_sem=send_sem.at[chunk, 8], recv_sem=recv_sem.at[chunk, 8],
            device_id=cell_target((place_in_cell + 1) % cell),
            device_id_type=pl.DeviceIdType.MESH,
        )

    def packed0(chunk):
        axis, other = route(chunk)
        n_outer, n_inner = highs[axis], highs[other]
        rows = n_outer * n_inner
        for state in range(2):
            pltpu.make_async_copy(
                store.at[state, chunk], sv.at[chunk, state], own_sem.at[chunk, state]
            ).wait()
        for index in range(cell):
            inner = {"group": index % LOW["group"], "owner": index // LOW["group"]}
            for state in range(2):
                for outer in range(n_outer):
                    first = (outer * LOW[axis] + inner[axis]) * count[other] + inner[other]
                    s0[chunk, pl.ds((index * 2 + state) * rows + outer * n_inner, n_inner), :] = sv[
                        chunk, state, pl.ds(first, n_inner, stride=LOW[other]), :
                    ]

    def packed_start(chunk):
        rows = highs["group"] * highs["owner"]

        def go(step, carry):
            cell_copy(chunk, (place_in_cell + shift(step, cell)) % cell).start()
            return carry
        lax.fori_loop(0, cell - 1, go, 0)
        mine = pl.ds(pl.multiple_of(place_in_cell * 2 * rows, 8), 2 * rows)
        r0[chunk, mine] = s0[chunk, mine]

    def packed1(chunk):
        axis, other = route(chunk)
        n_outer, n_inner = highs[axis], highs[other]
        rows = n_outer * n_inner
        await_cell(chunk, r0).wait_recv()
        for outer in range(n_outer):
            held = jnp.concatenate(
                [r0[chunk, pl.ds(i * rows + outer * n_inner, n_inner), :] for i in range(2 * cell)],
                axis=0,
            )
            t0[chunk, pl.ds(outer * CELL * n_inner, CELL * n_inner), :] = dot_exact(mk[...], held)
        send_high(chunk, 0, axis, t0, r1, CELL * n_inner)

    def packed2(chunk):
        axis, other = route(chunk)
        n_outer, n_inner = highs[axis], highs[other]
        await_high(chunk, 0, axis, r1, CELL * n_inner).wait_recv()
        for inner in range(n_inner):
            held = r1[chunk, pl.ds(inner, n_outer * CELL, stride=n_inner), :]
            t1[chunk, pl.ds(inner * PLANE, PLANE), :] = dot_exact(mf[chunk % 2], held)
        send_high(chunk, 1, other, t1, r2, PLANE)

    def packed3(chunk):
        axis, other = route(chunk)
        await_high(chunk, 1, other, r2, PLANE).wait_recv()
        select(chunk, m1, r2, w3)
        send(chunk, 2, other, w3, r3, count[axis])
        keep(chunk, other, w3, r3, count[axis])

    def stage1(chunk):
        axis, other = route(chunk)
        rows = count[other]

        def go(step, carry):
            target = turn(axis, step)
            for state in range(2):
                remote(
                    axis,
                    store.at[state, chunk, pl.ds(pl.multiple_of(target * rows, 8), rows)],
                    r1.at[chunk, pl.ds(pl.multiple_of((me[axis] * 2 + state) * rows, 8), rows)],
                    chunk, 0, target,
                ).start()
            return carry
        lax.fori_loop(0, count[axis] - 1, go, 0)
        for state in range(2):
            pltpu.make_async_copy(
                store.at[state, chunk, pl.ds(pl.multiple_of(me[axis] * rows, 8), rows)],
                r1.at[chunk, pl.ds(pl.multiple_of((me[axis] * 2 + state) * rows, 8), rows)],
                own_sem.at[chunk, state],
            ).start()

    def stage2(chunk):
        axis, other = route(chunk)
        rows = count[other]
        for state in range(2):
            pltpu.make_async_copy(
                store.at[state, chunk, pl.ds(pl.multiple_of(me[axis] * rows, 8), rows)],
                r1.at[chunk, pl.ds(pl.multiple_of((me[axis] * 2 + state) * rows, 8), rows)],
                own_sem.at[chunk, state],
            ).wait()
        await_recv(chunk, 0, axis, r1, 2 * rows)
        regroup(chunk, r1, t1, 2 * count[axis], rows)
        send(chunk, 1, other, t1, r2, 2 * count[axis])
        keep(chunk, other, t1, r2, 2 * count[axis])

    def stage3(chunk):
        axis, other = route(chunk)
        await_recv(chunk, 1, other, r2, 2 * count[axis])
        select(chunk, m1, r2, w3)
        send(chunk, 2, other, w3, r3, count[axis])
        keep(chunk, other, w3, r3, count[axis])

    def stage4(chunk):
        axis, other = route(chunk)
        await_recv(chunk, 2, other, r3, count[axis])
        regroup(chunk, r3, t3, count[other], count[axis])
        send(chunk, 3, axis, t3, r4, count[other])
        keep(chunk, axis, t3, r4, count[other])

    def stage5(chunk):
        axis, other = route(chunk)
        await_recv(chunk, 3, axis, r4, count[other])
        advance(chunk)
        send(chunk, 4, axis, fin, r5, count[other])
        keep(chunk, axis, fin, r5, count[other])

    def stage6(chunk):
        axis, other = route(chunk)
        await_recv(chunk, 4, axis, r5, count[other])
        regroup(chunk, r5, t5, count[axis], count[other])
        send(chunk, 5, other, t5, r6, count[axis])
        keep(chunk, other, t5, r6, count[axis])

    def stage7(chunk):
        axis, other = route(chunk)
        await_recv(chunk, 5, other, r6, count[axis])
        select(chunk, m2, r6, w7)
        send(chunk, 6, other, w7, r7, count[axis])
        keep(chunk, other, w7, r7, count[axis])

    def stage8(chunk):
        axis, other = route(chunk)
        await_recv(chunk, 6, other, r7, count[axis])
        regroup(chunk, r7, t7, count[other], count[axis])
        send(chunk, 7, axis, t7, ckpt, count[other])
        keep(chunk, axis, t7, ckpt, count[other])

    def stage9(chunk):
        axis, other = route(chunk)
        await_recv(chunk, 7, axis, ckpt, count[other])

    def index_matrices():
        strip = 128
        hit_row, slot_row = hit[...], slot[...]

        def swap(x):
            return (x % groups) * owners + x // groups

        slot_swapped = jnp.zeros((1, total), jnp.int32)
        for first in range(0, total, strip):
            place = pl.ds(first, strip)
            row = iota((strip, total), 0) + first
            lane = iota((strip, total), 1)
            hit_natural = pick(row == lane, hit_row, 1)
            hit_swapped = pick(swap(row) == lane, hit_row, 1)
            slot_natural = pick(row == lane, slot_row, 1)
            slot_swapped = slot_swapped + pick(row == swap(lane), slot_natural, 0)
            state = iota((strip, 2 * total), 1)
            named = ((state // 2) % groups * owners + state // (2 * groups)) * 2 + state % 2
            one = jnp.ones((), F32)
            zero = jnp.zeros((), F32)
            m1[0, place, :] = jnp.where(hit_swapped == named, one, zero).astype(BF16)
            m1[1, place, :] = jnp.where(hit_natural == state, one, zero).astype(BF16)
            m2[1, place, :] = jnp.where(slot_row == row, one, zero).astype(BF16)
        for first in range(0, total, strip):
            row = iota((strip, total), 0) + first
            m2[0, pl.ds(first, strip), :] = jnp.where(
                slot_swapped == swap(row), one, zero
            ).astype(BF16)

    def packed_matrices():
        strip = 128
        n_y, n_z = highs["group"], highs["owner"]
        held = 2 * cell
        lanes = n_z * held
        one = jnp.ones((), F32)
        zero = jnp.zeros((), F32)

        def mark(mask):
            return jnp.where(mask, one, zero)

        def swap(x):
            return (x % groups) * owners + x // groups

        hit_row, slot_row = hit[...], slot[...]
        slot_swapped = jnp.zeros((1, total), jnp.int32)
        for first in range(0, total, strip):
            place = pl.ds(first, strip)
            row = iota((strip, total), 0) + first
            lane = iota((strip, total), 1)
            spread = (strip, lanes)
            hc[0, place, :] = jnp.broadcast_to(pick(swap(row) == lane, hit_row, 1), spread)
            hc[1, place, :] = jnp.broadcast_to(pick(row == lane, hit_row, 1), spread)
            slot_natural = pick(row == lane, slot_row, 1)
            slot_swapped = slot_swapped + pick(row == swap(lane), slot_natural, 0)
            m2[1, place, :] = mark(slot_row == row).astype(BF16)
        for first in range(0, total, strip):
            row = iota((strip, total), 0) + first
            m2[0, pl.ds(first, strip), :] = mark(slot_swapped == swap(row)).astype(BF16)

        lane = iota((1, lanes), 1)
        in_cell = lane % held
        owner_of = lane // held * LOW["owner"] + in_cell // (2 * LOW["group"])
        core_of = in_cell // 2 % LOW["group"]
        names = [
            ((y * LOW["group"] + core_of) * owners + owner_of) * 2 + lane % 2 for y in range(n_y)
        ]
        present = jnp.concatenate(
            [jnp.max(mark(hc[1] == name), axis=0, keepdims=True) for name in names], axis=0
        )
        a, b = iota((lanes, lanes), 0), iota((lanes, lanes), 1)
        here = present.astype(BF16)
        rank = dot(here, mark((a // held == b // held) & (a < b)).astype(BF16))
        number = dot(here, mark(a // held == b // held).astype(BF16))
        before_z = dot(here, mark(a // held < b // held).astype(BF16))
        running = jnp.zeros((1, lanes), F32)
        before = []
        for y in range(n_y):
            before.append(running)
            running = running + number[y : y + 1]
        before_y = jnp.concatenate(before, axis=0)
        own_row = iota((n_y, lanes), 0)
        z_of = (iota((n_y, lanes), 1) // held).astype(F32)
        place_in = (
            z_of * PLANE + before_y + rank,
            own_row.astype(F32) * PLANE + before_z + rank,
        )
        excess = jnp.maximum(
            jnp.max(number - CELL, axis=(0, 1), keepdims=True),
            jnp.maximum(
                jnp.max(running - PLANE, axis=(0, 1), keepdims=True),
                jnp.max(before_z + number - PLANE, axis=(0, 1), keepdims=True),
            ),
        )
        flag[0, 0] = jnp.max(excess)

        for way, n_parts in ((0, n_z), (1, n_y)):
            for first in range(0, total, strip):
                rows = pl.ds(first, strip)
                wanted = hc[way, rows, :]
                found = jnp.zeros((strip, lanes), F32)
                for y, name in enumerate(names):
                    found = found + jnp.where(wanted == name, place_in[way][y : y + 1], zero)
                found = jnp.sum(found, axis=1, keepdims=True)
                table = iota((strip, n_parts * PLANE), 1).astype(F32)
                m1[way, rows, :] = mark(found == table).astype(BF16)

        n_inner = lanes // held
        mine = pick(own_row == high["group"], present * (rank + one), 0)
        a, b = iota((lanes, held * n_inner), 0), iota((lanes, held * n_inner), 1)
        own_cell = (a // held == high["owner"]) & (a % held == b // n_inner)
        entry = dot(
            jnp.broadcast_to(mine, (8, lanes)).astype(BF16), mark(own_cell).astype(BF16)
        )[:1]
        shape = (CELL * n_inner, held * n_inner)
        row, col = iota(shape, 0), iota(shape, 1)
        mk[...] = mark(
            (entry == (row // n_inner + 1).astype(F32)) & (row % n_inner == col % n_inner)
        ).astype(BF16)

        def fill(way, base, amount, n_parts):
            shape = (PLANE, n_parts * CELL)
            row = iota(shape, 0).astype(F32)
            nth = (iota((1, n_parts * CELL), 1) % CELL).astype(F32)
            mf[way] = mark((base + nth == row) & (nth < amount)).astype(BF16)

        own_lane = iota((n_y, lanes), 1) == high["owner"] * held
        sub, lane = iota((n_y, n_y * CELL), 0), iota((n_y, n_y * CELL), 1)
        spread_y = [
            pick(sub == lane // CELL, jnp.broadcast_to(pick(own_lane, x, 1), sub.shape), 0)
            for x in (before_y, number)
        ]
        fill(0, *spread_y, n_y)
        a, b = iota((lanes, n_z * CELL), 0), iota((lanes, n_z * CELL), 1)
        expand = mark(a == b // CELL * held).astype(BF16)
        spread_z = [
            dot(
                jnp.broadcast_to(
                    pick(own_row == high["group"], x, 0), (8, lanes)
                ).astype(BF16),
                expand,
            )[:1]
            for x in (before_z, number)
        ]
        fill(1, *spread_z, n_z)

    square = (length, length)

    def same(size):
        return iota(square, 0) // size == iota(square, 1) // size

    def turned(x):
        padded = jnp.concatenate([x, jnp.zeros((length - heads, length), F32)], axis=0)
        return padded.T[:, :heads]

    def cumulate():
        lower = (iota(square, 0) >= iota(square, 1)) & same(SPAN)
        ones = jnp.where(lower, jnp.ones((), F32), jnp.zeros((), F32))
        cum = jnp.dot(
            ones, turned(ld[...]), precision=lax.Precision.HIGHEST, preferred_element_type=F32
        )
        cum_ref[...] = cum
        padded = jnp.concatenate([cum, jnp.zeros((length, length - heads), F32)], axis=1)
        cumt_ref[...] = padded.T[:heads]
        rate_ref[...] = turned(wr[...])

    def prepare(chunk, carry):
        row, col = iota(square, 0), iota(square, 1)
        eye = row == col
        lower = (row >= col) & same(SPAN)
        strict = (row > col) & same(SPAN)
        unit = jnp.where(eye, jnp.ones((), F32), jnp.zeros((), F32))
        lane = iota((length, heads), 1)
        key_dim = q.shape[1] // key_heads
        amats = []
        for inner in range(per_chunk // repeat):
            key_head = chunk * (per_chunk // repeat) + inner
            place = pl.ds(pl.multiple_of(key_head * key_dim, 128), key_dim)
            key, query = k[:, place], q[:, place]
            trans = (((1,), (1,)), ((), ()))
            gram = lax.dot_general(key, key, trans, preferred_element_type=F32)
            cross = lax.dot_general(query, key, trans, preferred_element_type=F32)
            key_col = lax.rsqrt(pick(eye, gram, 1) + 1e-06)
            key_row = lax.rsqrt(pick(eye, gram, 0) + 1e-06)
            query32 = query.astype(F32)
            query_col = lax.rsqrt(
                jnp.sum(query32 * query32, axis=1, keepdims=True) + 1e-06
            ) * key_dim ** (-0.5)
            gram = gram * key_col * key_row
            cross = cross * query_col * key_row
            for extra in range(repeat):
                head = key_head * repeat + extra
                cum_col = pick(lane == head, cum_ref[...], 1)
                rate_col = pick(lane == head, rate_ref[...], 1)
                gap = cum_col - cumt_ref[pl.ds(head, 1), :]
                decay = jnp.where(lower, jnp.exp(jnp.where(lower, gap, 0.0)), 0.0)
                sco[head] = wide(cross * decay)
                amats.append((head, jnp.where(strict, rate_col * gram * decay, 0.0)))
        results = []
        small = 8
        within = same(small)
        diag = [jnp.where(within, a, 0.0) for _, a in amats]
        xs = [unit - b for b in diag]
        for _ in range(2):
            diag = [dot_full(b, b) for b in diag]
            xs = [x + dot_full(x, b) for x, b in zip(xs, diag)]
        size = small
        while size < SPAN:
            cross_mask = same(2 * size) & ~same(size)
            parts = [jnp.where(cross_mask, a, 0.0) for _, a in amats]
            inner_products = [dot_full(p, x) for p, x in zip(parts, xs)]
            xs = [x - dot_full(x, p) for x, p in zip(xs, inner_products)]
            size *= 2
        for (head, _), x in zip(amats, xs):
            inv[head] = wide(x)
        return carry

    def advance(chunk):
        key_dim = q.shape[1] // key_heads
        value_dim = v.shape[1] // heads
        head_list = [chunk * per_chunk + i for i in range(per_chunk)]
        states = [r4[chunk, pl.ds(i * key_dim, key_dim), :] for i in range(per_chunk)]
        for first in range(0, length, SPAN):
            rows = pl.ds(first, SPAN)
            block = (first, first + SPAN)
            reads, scales = [], []
            for i, head in enumerate(head_list):
                cols = pl.ds(head // repeat * key_dim, key_dim)
                both = jnp.concatenate([k[rows, cols], q[rows, cols]], axis=0)
                reads.append(dot_exact(both, states[i]))
            news = []
            for i, head in enumerate(head_list):
                cols = pl.ds(head // repeat * key_dim, key_dim)
                key32 = k[rows, cols].astype(F32)
                query32 = q[rows, cols].astype(F32)
                key_scale = lax.rsqrt(jnp.sum(key32 * key32, axis=1, keepdims=True) + 1e-06)
                query_scale = lax.rsqrt(
                    jnp.sum(query32 * query32, axis=1, keepdims=True) + 1e-06
                ) * key_dim ** (-0.5)
                cum_col = cum_ref[rows, head : head + 1]
                last = cum_ref[pl.ds(first + SPAN - 1, 1), head : head + 1]
                grown = jnp.exp(cum_col)
                rate = rate_ref[rows, head : head + 1]
                value = v[rows, pl.ds(head * value_dim, value_dim)].astype(F32)
                rest = rate * (value - (grown * key_scale) * reads[i][:SPAN])
                matrix = inv[head, rows, :]
                left = jnp.concatenate(
                    [matrix[:, first : first + SPAN],
                     matrix[:, length + first : length + first + SPAN]], axis=1
                )
                news.append(dot_pair(left, rest))
                scales.append((query_scale * grown, key_scale * jnp.exp(last - cum_col), jnp.exp(last)))
            for i, head in enumerate(head_list):
                cols = pl.ds(head // repeat * key_dim, key_dim)
                query_scale, key_scale, tail = scales[i]
                matrix = sco[head, rows, :]
                left = jnp.concatenate(
                    [matrix[:, first : first + SPAN],
                     matrix[:, length + first : length + first + SPAN]], axis=1
                )
                result = query_scale * reads[i][SPAN:] + dot_pair(left, news[i])
                out[rows, pl.ds(head * value_dim, value_dim)] = result.astype(out.dtype)
                key_t = k[rows, cols].T
                states[i] = tail * states[i] + dot_exact(key_t, key_scale * news[i])
        for i in range(per_chunk):
            fin[chunk, pl.ds(i * key_dim, key_dim), :] = states[i]

    if packed:
        for chunk in range(chunks):
            packed0(chunk)
        packed_matrices()
        cumulate()
        pl.semaphore_wait(barrier, greeted)
        for chunk in range(chunks):
            packed_start(chunk)
        prepare(0, 0)
        packed1(0)
        packed1(1)
        prepare(1, 0)
        lead = [packed2, packed3]
    else:
        pl.semaphore_wait(barrier, greeted)
        stage1(0)
        stage1(1)
        index_matrices()
        cumulate()
        lax.fori_loop(0, chunks, prepare, 0)
        stage1(2)
        stage1(3)
        lead = [stage2, stage3]
    lead = lead + [stage4, stage5, stage6, stage7, stage8, stage9]
    ahead, behind = (0, 1), (2, 3)
    for step in range(len(lead) + 1):
        if step < len(lead):
            for chunk in ahead:
                lead[step](chunk)
        if step == 0 and packed:
            for chunk in behind:
                packed1(chunk)
            prepare(2, 0)
        if step == 1 and packed:
            prepare(3, 0)
        if step >= 1:
            for chunk in behind:
                lead[step - 1](chunk)
    for chunk in range(chunks):
        axis, other = route(chunk)
        na, nb = count[axis], count[other]
        if packed:
            await_cell(chunk, s0).wait_send()
            await_high(chunk, 0, axis, t0, CELL * highs[other]).wait_send()
            await_high(chunk, 1, other, t1, PLANE).wait_send()
        else:
            await_send(chunk, 0, axis, r1, 2 * nb)
            await_send(chunk, 1, other, t1, 2 * na)
        await_send(chunk, 2, other, w3, na)
        await_send(chunk, 3, axis, t3, nb)
        await_send(chunk, 4, axis, fin, nb)
        await_send(chunk, 5, other, t5, na)
        await_send(chunk, 6, other, w7, na)
        await_send(chunk, 7, axis, t7, nb)


def run(packed, prefix_store, queries, key_rows, values, log_decay, write_rate, hit_state, save_slot):
    groups = lax.axis_size("group")
    owners = lax.axis_size("owner")
    slots, heads, key_dim, value_dim = prefix_store.shape
    total = groups * owners
    length = queries.shape[0]
    key_heads = queries.shape[1] // key_dim
    chunks = heads * key_dim // total
    vmem = pl.BlockSpec(memory_space=pltpu.VMEM)
    anywhere = pl.BlockSpec(memory_space=pl.ANY)

    def buffer(rows):
        return pltpu.VMEM((chunks, rows, value_dim), F32)

    out_shape = [
        jax.ShapeDtypeStruct((length, heads * value_dim), BF16),
        jax.ShapeDtypeStruct((chunks, total, value_dim), F32),
    ]
    out_specs = [vmem, vmem]
    scratch = []
    if packed:
        cell = LOW["group"] * LOW["owner"]
        n_y, n_z = groups // LOW["group"], owners // LOW["owner"]
        assert n_y == n_z == 8 and cell == 8 and n_z * 2 * cell == 128
        out_shape.append(jax.ShapeDtypeStruct((1, 1), F32))
        out_specs.append(pl.BlockSpec(memory_space=pltpu.SMEM))
        scratch = [
            pltpu.VMEM((chunks, 2, total, value_dim), F32),
            buffer(2 * total), buffer(2 * total), buffer(n_y * n_z * CELL),
            pltpu.VMEM((2, total, 128), jnp.int32),
            pltpu.VMEM((CELL * n_z, 2 * cell * n_z), BF16),
            pltpu.VMEM((2, PLANE, n_y * CELL), BF16),
        ]
        spread = [n_y * n_z * CELL, n_z * PLANE, n_z * PLANE]
    else:
        spread = [2 * total] * 3
    results = pl.pallas_call(
        functools.partial(kernel, packed, groups, owners, chunks, heads, key_heads, length),
        out_shape=out_shape,
        in_specs=[anywhere] + [vmem] * 7,
        out_specs=out_specs,
        scratch_shapes=scratch + [buffer(rows) for rows in spread] + [buffer(total)] * 11 + [
            pltpu.VMEM((2, total, spread[2]), BF16),
            pltpu.VMEM((2, total, total), BF16),
            pltpu.VMEM((heads, length, 2 * length), BF16),
            pltpu.VMEM((heads, length, 2 * length), BF16),
            pltpu.VMEM((length, heads), F32),
            pltpu.VMEM((heads, length), F32),
            pltpu.VMEM((length, heads), F32),
            pltpu.SemaphoreType.DMA((chunks, 9)),
            pltpu.SemaphoreType.DMA((chunks, 9)),
            pltpu.SemaphoreType.DMA((chunks, 2)),
        ],
        compiler_params=pltpu.CompilerParams(
            collective_id=0 if packed else 1, has_side_effects=True,
            vmem_limit_bytes=56 * 1024 * 1024,
        ),
        cost_estimate=pl.CostEstimate(
            flops=4 * 10**9, bytes_accessed=6 * 2**20, transcendentals=2**19
        ),
    )(
        prefix_store.reshape(slots, chunks, total, value_dim),
        queries, key_rows, values, log_decay.T, write_rate.T,
        hit_state.reshape(1, total), save_slot.reshape(1, total),
    )
    results = list(results)
    results[1] = results[1].reshape(1, heads, key_dim, value_dim)
    return results


def body(*args):
    head_output, checkpoints, excess = run(True, *args)
    return lax.cond(
        excess[0, 0] > 0,
        lambda operands, done: tuple(run(False, *operands)),
        lambda operands, done: done,
        args, (head_output, checkpoints),
    )


def solution(mesh):
    split_rows = P(("group", "owner"), None)
    split_states = P(("group", "owner"), None, None, None)
    in_specs = (split_states,) + (split_rows,) * 5 + (P(), P())
    return jax.shard_map(
        body, mesh=mesh, in_specs=in_specs, out_specs=(split_rows, split_states), check_vma=False
    )
```

```python
import functools

import jax
import jax.numpy as jnp
from jax import lax
from jax.experimental import pallas as pl
from jax.experimental.pallas import tpu as pltpu
from jax.sharding import PartitionSpec as P

SPAN = 64
F32 = jnp.float32
BF16 = jnp.bfloat16


def split(x):
    hi = x.astype(BF16)
    return hi, (x - hi.astype(F32)).astype(BF16)


def wide(x):
    return jnp.concatenate(split(x), axis=1)


def fold(x):
    half = x.shape[1] // 2
    return x[:, :half] + x[:, half:]


def dot(a, b):
    return lax.dot_general(a, b, (((1,), (0,)), ((), ())), preferred_element_type=F32)


def dot_exact(a, b):
    return fold(dot(a, wide(b)))


def dot_pair(a_wide, b):
    both = wide(b)
    return fold(dot(a_wide, jnp.concatenate([both, both], axis=0)))


def dot_full(a, b):
    return dot_pair(wide(a), b)


def iota(shape, dim):
    return lax.broadcasted_iota(jnp.int32, shape, dim)


def pick(mask, x, axis):
    return jnp.sum(jnp.where(mask, x, jnp.zeros_like(x)), axis=axis, keepdims=True)


LOW = {"group": 2, "owner": 4}
CELL, PLANE = 11, 48


def kernel(
    packed, groups, owners, chunks, heads, key_heads, length,
    store, q, k, v, ld, wr, hit, slot,
    *refs,
):
    if packed:
        out, ckpt, flag, *refs = refs
        sv, s0, r0, t0, hc, mk, mf, *refs = refs
    else:
        out, ckpt, *refs = refs
    (
        r1, t1, r2, w3, r3, t3, r4, fin, r5, t5, r6, w7, r7, t7,
        m1, m2, inv, sco, cum_ref, cumt_ref, rate_ref,
        send_sem, recv_sem, own_sem,
    ) = refs
    total = groups * owners
    me = {"group": lax.axis_index("group"), "owner": lax.axis_index("owner")}
    count = {"group": groups, "owner": owners}
    per_chunk = heads // chunks
    repeat = heads // key_heads

    def route(chunk):
        return ("group", "owner") if chunk % 2 == 0 else ("owner", "group")

    low = {axis: me[axis] % LOW[axis] for axis in me}
    high = {axis: me[axis] // LOW[axis] for axis in me}
    highs = {axis: count[axis] // LOW[axis] for axis in me}
    cell = LOW["group"] * LOW["owner"]
    place_in_cell = low["owner"] * LOW["group"] + low["group"]

    def shift(step, n):
        odd = step % 2
        return (1 - odd) * (step // 2 + 1) + odd * (n - (step + 1) // 2)

    def turn(axis, step):
        n, part = count[axis], LOW[axis]
        offset = shift(step, n)
        inner = (low[axis] + offset % part) % part
        outer = (high[axis] + offset // part) % (n // part)
        return outer * part + inner

    def turn_high(axis, step):
        return (high[axis] + shift(step, highs[axis])) % highs[axis]

    def cell_target(index):
        return {
            "group": high["group"] * LOW["group"] + index % LOW["group"],
            "owner": high["owner"] * LOW["owner"] + index // LOW["group"],
        }

    if packed:
        for chunk in range(chunks):
            for state in range(2):
                pltpu.make_async_copy(
                    store.at[state, chunk], sv.at[chunk, state], own_sem.at[chunk, state]
                ).start()

    barrier = pltpu.get_barrier_semaphore()
    for axis in ("group", "owner"):
        def greet(step, carry, axis=axis):
            pl.semaphore_signal(
                barrier, inc=1, device_id={axis: turn(axis, step)},
                device_id_type=pl.DeviceIdType.MESH,
            )
            return carry
        lax.fori_loop(0, count[axis] - 1, greet, 0)
    greeted = groups + owners - 2
    if packed:
        def greet_cell(step, carry):
            inner = (low["owner"] + step + 1) % LOW["owner"]
            pl.semaphore_signal(
                barrier, inc=1,
                device_id=cell_target(inner * LOW["group"] + 1 - low["group"]),
                device_id_type=pl.DeviceIdType.MESH,
            )
            return carry
        lax.fori_loop(0, LOW["owner"] - 1, greet_cell, 0)
        greeted = greeted + LOW["owner"] - 1

    def remote(axis, src, dst, chunk, stage, target):
        return pltpu.make_async_remote_copy(
            src_ref=src, dst_ref=dst,
            send_sem=send_sem.at[chunk, stage], recv_sem=recv_sem.at[chunk, stage],
            device_id={axis: target}, device_id_type=pl.DeviceIdType.MESH,
        )

    def send(chunk, stage, axis, src, dst, rows):
        def go(step, carry):
            target = turn(axis, step)
            remote(
                axis,
                src.at[chunk, pl.ds(pl.multiple_of(target * rows, 8), rows)],
                dst.at[chunk, pl.ds(pl.multiple_of(me[axis] * rows, 8), rows)],
                chunk, stage, target,
            ).start()
            return carry
        lax.fori_loop(0, count[axis] - 1, go, 0)

    def keep(chunk, axis, src, dst, rows):
        place = pl.ds(pl.multiple_of(me[axis] * rows, 8), rows)
        dst[chunk, place] = src[chunk, place]

    def await_recv(chunk, stage, axis, dst, rows):
        part = dst.at[chunk, pl.ds(0, (count[axis] - 1) * rows)]
        remote(axis, part, part, chunk, stage, turn(axis, 0)).wait_recv()

    def await_send(chunk, stage, axis, src, rows):
        part = src.at[chunk, pl.ds(0, (count[axis] - 1) * rows)]
        remote(axis, part, part, chunk, stage, turn(axis, 0)).wait_send()

    def regroup(chunk, src, dst, n_outer, n_inner):
        for inner in range(n_inner):
            dst[chunk, pl.ds(inner * n_outer, n_outer), :] = src[
                chunk, pl.ds(inner, n_outer, stride=n_inner), :
            ]

    def select(chunk, matrix, src, dst):
        rows = src.shape[1]
        both = wide(src[chunk])
        strip = 128
        for first in range(0, total, strip):
            dst[chunk, pl.ds(first, strip), :] = fold(
                dot(matrix[chunk % 2, pl.ds(first, strip), :], both)
            )

    def send_high(chunk, stage, axis, src, dst, rows):
        def go(step, carry):
            target = turn_high(axis, step)
            remote(
                axis,
                src.at[chunk, pl.ds(pl.multiple_of(target * rows, 8), rows)],
                dst.at[chunk, pl.ds(pl.multiple_of(high[axis] * rows, 8), rows)],
                chunk, stage, target * LOW[axis] + low[axis],
            ).start()
            return carry
        lax.fori_loop(0, highs[axis] - 1, go, 0)
        mine = pl.ds(pl.multiple_of(high[axis] * rows, 8), rows)
        dst[chunk, mine] = src[chunk, mine]

    def await_high(chunk, stage, axis, dst, rows):
        part = dst.at[chunk, pl.ds(0, (highs[axis] - 1) * rows)]
        copy = remote(axis, part, part, chunk, stage, turn(axis, 0))
        return copy

    def cell_copy(chunk, target):
        rows = 2 * highs["group"] * highs["owner"]
        return pltpu.make_async_remote_copy(
            src_ref=s0.at[chunk, pl.ds(pl.multiple_of(target * rows, 8), rows)],
            dst_ref=r0.at[chunk, pl.ds(pl.multiple_of(place_in_cell * rows, 8), rows)],
            send_sem=send_sem.at[chunk, 8], recv_sem=recv_sem.at[chunk, 8],
            device_id=cell_target(target), device_id_type=pl.DeviceIdType.MESH,
        )

    def await_cell(chunk, ref):
        rows = 2 * highs["group"] * highs["owner"]
        part = ref.at[chunk, pl.ds(0, (cell - 1) * rows)]
        return pltpu.make_async_remote_copy(
            src_ref=part, dst_ref=part,
            send_sem=send_sem.at[chunk, 8], recv_sem=recv_sem.at[chunk, 8],
            device_id=cell_target((place_in_cell + 1) % cell),
            device_id_type=pl.DeviceIdType.MESH,
        )

    def packed0(chunk):
        axis, other = route(chunk)
        n_outer, n_inner = highs[axis], highs[other]
        rows = n_outer * n_inner
        for state in range(2):
            pltpu.make_async_copy(
                store.at[state, chunk], sv.at[chunk, state], own_sem.at[chunk, state]
            ).wait()
        for index in range(cell):
            inner = {"group": index % LOW["group"], "owner": index // LOW["group"]}
            for state in range(2):
                for outer in range(n_outer):
                    first = (outer * LOW[axis] + inner[axis]) * count[other] + inner[other]
                    s0[chunk, pl.ds((index * 2 + state) * rows + outer * n_inner, n_inner), :] = sv[
                        chunk, state, pl.ds(first, n_inner, stride=LOW[other]), :
                    ]

    def packed_start(chunk):
        rows = highs["group"] * highs["owner"]

        def go(step, carry):
            cell_copy(chunk, (place_in_cell + shift(step, cell)) % cell).start()
            return carry
        lax.fori_loop(0, cell - 1, go, 0)
        mine = pl.ds(pl.multiple_of(place_in_cell * 2 * rows, 8), 2 * rows)
        r0[chunk, mine] = s0[chunk, mine]

    def packed1(chunk):
        axis, other = route(chunk)
        n_outer, n_inner = highs[axis], highs[other]
        rows = n_outer * n_inner
        await_cell(chunk, r0).wait_recv()
        for outer in range(n_outer):
            held = jnp.concatenate(
                [r0[chunk, pl.ds(i * rows + outer * n_inner, n_inner), :] for i in range(2 * cell)],
                axis=0,
            )
            t0[chunk, pl.ds(outer * CELL * n_inner, CELL * n_inner), :] = dot_exact(mk[...], held)
        send_high(chunk, 0, axis, t0, r1, CELL * n_inner)

    def packed2(chunk):
        axis, other = route(chunk)
        n_outer, n_inner = highs[axis], highs[other]
        await_high(chunk, 0, axis, r1, CELL * n_inner).wait_recv()
        for inner in range(n_inner):
            held = r1[chunk, pl.ds(inner, n_outer * CELL, stride=n_inner), :]
            t1[chunk, pl.ds(inner * PLANE, PLANE), :] = dot_exact(mf[chunk % 2], held)
        send_high(chunk, 1, other, t1, r2, PLANE)

    def packed3(chunk):
        axis, other = route(chunk)
        await_high(chunk, 1, other, r2, PLANE).wait_recv()
        select(chunk, m1, r2, w3)
        send(chunk, 2, other, w3, r3, count[axis])
        keep(chunk, other, w3, r3, count[axis])

    def stage1(chunk):
        axis, other = route(chunk)
        rows = count[other]

        def go(step, carry):
            target = turn(axis, step)
            for state in range(2):
                remote(
                    axis,
                    store.at[state, chunk, pl.ds(pl.multiple_of(target * rows, 8), rows)],
                    r1.at[chunk, pl.ds(pl.multiple_of((me[axis] * 2 + state) * rows, 8), rows)],
                    chunk, 0, target,
                ).start()
            return carry
        lax.fori_loop(0, count[axis] - 1, go, 0)
        for state in range(2):
            pltpu.make_async_copy(
                store.at[state, chunk, pl.ds(pl.multiple_of(me[axis] * rows, 8), rows)],
                r1.at[chunk, pl.ds(pl.multiple_of((me[axis] * 2 + state) * rows, 8), rows)],
                own_sem.at[chunk, state],
            ).start()

    def stage2(chunk):
        axis, other = route(chunk)
        rows = count[other]
        for state in range(2):
            pltpu.make_async_copy(
                store.at[state, chunk, pl.ds(pl.multiple_of(me[axis] * rows, 8), rows)],
                r1.at[chunk, pl.ds(pl.multiple_of((me[axis] * 2 + state) * rows, 8), rows)],
                own_sem.at[chunk, state],
            ).wait()
        await_recv(chunk, 0, axis, r1, 2 * rows)
        regroup(chunk, r1, t1, 2 * count[axis], rows)
        send(chunk, 1, other, t1, r2, 2 * count[axis])
        keep(chunk, other, t1, r2, 2 * count[axis])

    def stage3(chunk):
        axis, other = route(chunk)
        await_recv(chunk, 1, other, r2, 2 * count[axis])
        select(chunk, m1, r2, w3)
        send(chunk, 2, other, w3, r3, count[axis])
        keep(chunk, other, w3, r3, count[axis])

    def stage4(chunk):
        axis, other = route(chunk)
        await_recv(chunk, 2, other, r3, count[axis])
        regroup(chunk, r3, t3, count[other], count[axis])
        send(chunk, 3, axis, t3, r4, count[other])
        keep(chunk, axis, t3, r4, count[other])

    def stage5(chunk):
        axis, other = route(chunk)
        await_recv(chunk, 3, axis, r4, count[other])
        advance(chunk)
        send(chunk, 4, axis, fin, r5, count[other])
        keep(chunk, axis, fin, r5, count[other])

    def stage6(chunk):
        axis, other = route(chunk)
        await_recv(chunk, 4, axis, r5, count[other])
        regroup(chunk, r5, t5, count[axis], count[other])
        send(chunk, 5, other, t5, r6, count[axis])
        keep(chunk, other, t5, r6, count[axis])

    def stage7(chunk):
        axis, other = route(chunk)
        await_recv(chunk, 5, other, r6, count[axis])
        select(chunk, m2, r6, w7)
        send(chunk, 6, other, w7, r7, count[axis])
        keep(chunk, other, w7, r7, count[axis])

    def stage8(chunk):
        axis, other = route(chunk)
        await_recv(chunk, 6, other, r7, count[axis])
        regroup(chunk, r7, t7, count[other], count[axis])
        send(chunk, 7, axis, t7, ckpt, count[other])
        keep(chunk, axis, t7, ckpt, count[other])

    def stage9(chunk):
        axis, other = route(chunk)
        await_recv(chunk, 7, axis, ckpt, count[other])

    def index_matrices():
        strip = 128
        hit_row, slot_row = hit[...], slot[...]

        def swap(x):
            return (x % groups) * owners + x // groups

        slot_swapped = jnp.zeros((1, total), jnp.int32)
        for first in range(0, total, strip):
            place = pl.ds(first, strip)
            row = iota((strip, total), 0) + first
            lane = iota((strip, total), 1)
            hit_natural = pick(row == lane, hit_row, 1)
            hit_swapped = pick(swap(row) == lane, hit_row, 1)
            slot_natural = pick(row == lane, slot_row, 1)
            slot_swapped = slot_swapped + pick(row == swap(lane), slot_natural, 0)
            state = iota((strip, 2 * total), 1)
            named = ((state // 2) % groups * owners + state // (2 * groups)) * 2 + state % 2
            one = jnp.ones((), F32)
            zero = jnp.zeros((), F32)
            m1[0, place, :] = jnp.where(hit_swapped == named, one, zero).astype(BF16)
            m1[1, place, :] = jnp.where(hit_natural == state, one, zero).astype(BF16)
            m2[1, place, :] = jnp.where(slot_row == row, one, zero).astype(BF16)
        for first in range(0, total, strip):
            row = iota((strip, total), 0) + first
            m2[0, pl.ds(first, strip), :] = jnp.where(
                slot_swapped == swap(row), one, zero
            ).astype(BF16)

    def packed_matrices():
        strip = 128
        n_y, n_z = highs["group"], highs["owner"]
        held = 2 * cell
        lanes = n_z * held
        one = jnp.ones((), F32)
        zero = jnp.zeros((), F32)

        def mark(mask):
            return jnp.where(mask, one, zero)

        def swap(x):
            return (x % groups) * owners + x // groups

        hit_row, slot_row = hit[...], slot[...]
        slot_swapped = jnp.zeros((1, total), jnp.int32)
        for first in range(0, total, strip):
            place = pl.ds(first, strip)
            row = iota((strip, total), 0) + first
            lane = iota((strip, total), 1)
            spread = (strip, lanes)
            hc[0, place, :] = jnp.broadcast_to(pick(swap(row) == lane, hit_row, 1), spread)
            hc[1, place, :] = jnp.broadcast_to(pick(row == lane, hit_row, 1), spread)
            slot_natural = pick(row == lane, slot_row, 1)
            slot_swapped = slot_swapped + pick(row == swap(lane), slot_natural, 0)
            m2[1, place, :] = mark(slot_row == row).astype(BF16)
        for first in range(0, total, strip):
            row = iota((strip, total), 0) + first
            m2[0, pl.ds(first, strip), :] = mark(slot_swapped == swap(row)).astype(BF16)

        lane = iota((1, lanes), 1)
        in_cell = lane % held
        owner_of = lane // held * LOW["owner"] + in_cell // (2 * LOW["group"])
        core_of = in_cell // 2 % LOW["group"]
        names = [
            ((y * LOW["group"] + core_of) * owners + owner_of) * 2 + lane % 2 for y in range(n_y)
        ]
        present = jnp.concatenate(
            [jnp.max(mark(hc[1] == name), axis=0, keepdims=True) for name in names], axis=0
        )
        a, b = iota((lanes, lanes), 0), iota((lanes, lanes), 1)
        here = present.astype(BF16)
        rank = dot(here, mark((a // held == b // held) & (a < b)).astype(BF16))
        number = dot(here, mark(a // held == b // held).astype(BF16))
        before_z = dot(here, mark(a // held < b // held).astype(BF16))
        running = jnp.zeros((1, lanes), F32)
        before = []
        for y in range(n_y):
            before.append(running)
            running = running + number[y : y + 1]
        before_y = jnp.concatenate(before, axis=0)
        own_row = iota((n_y, lanes), 0)
        z_of = (iota((n_y, lanes), 1) // held).astype(F32)
        place_in = (
            z_of * PLANE + before_y + rank,
            own_row.astype(F32) * PLANE + before_z + rank,
        )
        excess = jnp.maximum(
            jnp.max(number - CELL, axis=(0, 1), keepdims=True),
            jnp.maximum(
                jnp.max(running - PLANE, axis=(0, 1), keepdims=True),
                jnp.max(before_z + number - PLANE, axis=(0, 1), keepdims=True),
            ),
        )
        flag[0, 0] = jnp.max(excess)

        for way, n_parts in ((0, n_z), (1, n_y)):
            for first in range(0, total, strip):
                rows = pl.ds(first, strip)
                wanted = hc[way, rows, :]
                found = jnp.zeros((strip, lanes), F32)
                for y, name in enumerate(names):
                    found = found + jnp.where(wanted == name, place_in[way][y : y + 1], zero)
                found = jnp.sum(found, axis=1, keepdims=True)
                table = iota((strip, n_parts * PLANE), 1).astype(F32)
                m1[way, rows, :] = mark(found == table).astype(BF16)

        n_inner = lanes // held
        mine = pick(own_row == high["group"], present * (rank + one), 0)
        a, b = iota((lanes, held * n_inner), 0), iota((lanes, held * n_inner), 1)
        own_cell = (a // held == high["owner"]) & (a % held == b // n_inner)
        entry = dot(
            jnp.broadcast_to(mine, (8, lanes)).astype(BF16), mark(own_cell).astype(BF16)
        )[:1]
        shape = (CELL * n_inner, held * n_inner)
        row, col = iota(shape, 0), iota(shape, 1)
        mk[...] = mark(
            (entry == (row // n_inner + 1).astype(F32)) & (row % n_inner == col % n_inner)
        ).astype(BF16)

        def fill(way, base, amount, n_parts):
            shape = (PLANE, n_parts * CELL)
            row = iota(shape, 0).astype(F32)
            nth = (iota((1, n_parts * CELL), 1) % CELL).astype(F32)
            mf[way] = mark((base + nth == row) & (nth < amount)).astype(BF16)

        own_lane = iota((n_y, lanes), 1) == high["owner"] * held
        sub, lane = iota((n_y, n_y * CELL), 0), iota((n_y, n_y * CELL), 1)
        spread_y = [
            pick(sub == lane // CELL, jnp.broadcast_to(pick(own_lane, x, 1), sub.shape), 0)
            for x in (before_y, number)
        ]
        fill(0, *spread_y, n_y)
        a, b = iota((lanes, n_z * CELL), 0), iota((lanes, n_z * CELL), 1)
        expand = mark(a == b // CELL * held).astype(BF16)
        spread_z = [
            dot(
                jnp.broadcast_to(
                    pick(own_row == high["group"], x, 0), (8, lanes)
                ).astype(BF16),
                expand,
            )[:1]
            for x in (before_z, number)
        ]
        fill(1, *spread_z, n_z)

    square = (length, length)

    def same(size):
        return iota(square, 0) // size == iota(square, 1) // size

    def turned(x):
        padded = jnp.concatenate([x, jnp.zeros((length - heads, length), F32)], axis=0)
        return padded.T[:, :heads]

    def cumulate():
        lower = (iota(square, 0) >= iota(square, 1)) & same(SPAN)
        ones = jnp.where(lower, jnp.ones((), F32), jnp.zeros((), F32))
        cum = jnp.dot(
            ones, turned(ld[...]), precision=lax.Precision.HIGHEST, preferred_element_type=F32
        )
        cum_ref[...] = cum
        padded = jnp.concatenate([cum, jnp.zeros((length, length - heads), F32)], axis=1)
        cumt_ref[...] = padded.T[:heads]
        rate_ref[...] = turned(wr[...])

    def prepare(chunk, carry):
        row, col = iota(square, 0), iota(square, 1)
        eye = row == col
        lower = (row >= col) & same(SPAN)
        strict = (row > col) & same(SPAN)
        unit = jnp.where(eye, jnp.ones((), F32), jnp.zeros((), F32))
        lane = iota((length, heads), 1)
        key_dim = q.shape[1] // key_heads
        amats = []
        for inner in range(per_chunk // repeat):
            key_head = chunk * (per_chunk // repeat) + inner
            place = pl.ds(pl.multiple_of(key_head * key_dim, 128), key_dim)
            key, query = k[:, place], q[:, place]
            trans = (((1,), (1,)), ((), ()))
            gram = lax.dot_general(key, key, trans, preferred_element_type=F32)
            cross = lax.dot_general(query, key, trans, preferred_element_type=F32)
            key_col = lax.rsqrt(pick(eye, gram, 1) + 1e-06)
            key_row = lax.rsqrt(pick(eye, gram, 0) + 1e-06)
            query32 = query.astype(F32)
            query_col = lax.rsqrt(
                jnp.sum(query32 * query32, axis=1, keepdims=True) + 1e-06
            ) * key_dim ** (-0.5)
            gram = gram * key_col * key_row
            cross = cross * query_col * key_row
            for extra in range(repeat):
                head = key_head * repeat + extra
                cum_col = pick(lane == head, cum_ref[...], 1)
                rate_col = pick(lane == head, rate_ref[...], 1)
                gap = cum_col - cumt_ref[pl.ds(head, 1), :]
                decay = jnp.where(lower, jnp.exp(jnp.where(lower, gap, 0.0)), 0.0)
                sco[head] = wide(cross * decay)
                amats.append((head, jnp.where(strict, rate_col * gram * decay, 0.0)))
        results = []
        small = 8
        within = same(small)
        diag = [jnp.where(within, a, 0.0) for _, a in amats]
        xs = [unit - b for b in diag]
        for _ in range(2):
            diag = [dot_full(b, b) for b in diag]
            xs = [x + dot_full(x, b) for x, b in zip(xs, diag)]
        size = small
        while size < SPAN:
            cross_mask = same(2 * size) & ~same(size)
            parts = [jnp.where(cross_mask, a, 0.0) for _, a in amats]
            inner_products = [dot_full(p, x) for p, x in zip(parts, xs)]
            xs = [x - dot_full(x, p) for x, p in zip(xs, inner_products)]
            size *= 2
        for (head, _), x in zip(amats, xs):
            inv[head] = wide(x)
        return carry

    def advance(chunk):
        key_dim = q.shape[1] // key_heads
        value_dim = v.shape[1] // heads
        head_list = [chunk * per_chunk + i for i in range(per_chunk)]
        states = [r4[chunk, pl.ds(i * key_dim, key_dim), :] for i in range(per_chunk)]
        for first in range(0, length, SPAN):
            rows = pl.ds(first, SPAN)
            block = (first, first + SPAN)
            reads, scales = [], []
            for i, head in enumerate(head_list):
                cols = pl.ds(head // repeat * key_dim, key_dim)
                both = jnp.concatenate([k[rows, cols], q[rows, cols]], axis=0)
                reads.append(dot_exact(both, states[i]))
            news = []
            for i, head in enumerate(head_list):
                cols = pl.ds(head // repeat * key_dim, key_dim)
                key32 = k[rows, cols].astype(F32)
                query32 = q[rows, cols].astype(F32)
                key_scale = lax.rsqrt(jnp.sum(key32 * key32, axis=1, keepdims=True) + 1e-06)
                query_scale = lax.rsqrt(
                    jnp.sum(query32 * query32, axis=1, keepdims=True) + 1e-06
                ) * key_dim ** (-0.5)
                cum_col = cum_ref[rows, head : head + 1]
                last = cum_ref[pl.ds(first + SPAN - 1, 1), head : head + 1]
                grown = jnp.exp(cum_col)
                rate = rate_ref[rows, head : head + 1]
                value = v[rows, pl.ds(head * value_dim, value_dim)].astype(F32)
                rest = rate * (value - (grown * key_scale) * reads[i][:SPAN])
                matrix = inv[head, rows, :]
                left = jnp.concatenate(
                    [matrix[:, first : first + SPAN],
                     matrix[:, length + first : length + first + SPAN]], axis=1
                )
                news.append(dot_pair(left, rest))
                scales.append((query_scale * grown, key_scale * jnp.exp(last - cum_col), jnp.exp(last)))
            for i, head in enumerate(head_list):
                cols = pl.ds(head // repeat * key_dim, key_dim)
                query_scale, key_scale, tail = scales[i]
                matrix = sco[head, rows, :]
                left = jnp.concatenate(
                    [matrix[:, first : first + SPAN],
                     matrix[:, length + first : length + first + SPAN]], axis=1
                )
                result = query_scale * reads[i][SPAN:] + dot_pair(left, news[i])
                out[rows, pl.ds(head * value_dim, value_dim)] = result.astype(out.dtype)
                key_t = k[rows, cols].T
                states[i] = tail * states[i] + dot_exact(key_t, key_scale * news[i])
        for i in range(per_chunk):
            fin[chunk, pl.ds(i * key_dim, key_dim), :] = states[i]

    if packed:
        for chunk in range(chunks):
            packed0(chunk)
        packed_matrices()
        cumulate()
        pl.semaphore_wait(barrier, greeted)
        for chunk in range(chunks):
            packed_start(chunk)
        prepare(0, 0)
        packed1(0)
        packed1(1)
        prepare(1, 0)
        lead = [packed2, packed3]
    else:
        pl.semaphore_wait(barrier, greeted)
        stage1(0)
        stage1(1)
        index_matrices()
        cumulate()
        lax.fori_loop(0, chunks, prepare, 0)
        stage1(2)
        stage1(3)
        lead = [stage2, stage3]
    lead = lead + [stage4, stage5, stage6, stage7, stage8, stage9]
    for step, stage in enumerate(lead):
        if packed and step == 0:
            packed1(2)
            packed1(3)
            prepare(2, 0)
        if packed and step == 1:
            prepare(3, 0)
        for chunk in range(chunks):
            stage(chunk)
    for chunk in range(chunks):
        axis, other = route(chunk)
        na, nb = count[axis], count[other]
        if packed:
            await_cell(chunk, s0).wait_send()
            await_high(chunk, 0, axis, t0, CELL * highs[other]).wait_send()
            await_high(chunk, 1, other, t1, PLANE).wait_send()
        else:
            await_send(chunk, 0, axis, r1, 2 * nb)
            await_send(chunk, 1, other, t1, 2 * na)
        await_send(chunk, 2, other, w3, na)
        await_send(chunk, 3, axis, t3, nb)
        await_send(chunk, 4, axis, fin, nb)
        await_send(chunk, 5, other, t5, na)
        await_send(chunk, 6, other, w7, na)
        await_send(chunk, 7, axis, t7, nb)


def run(packed, prefix_store, queries, key_rows, values, log_decay, write_rate, hit_state, save_slot):
    groups = lax.axis_size("group")
    owners = lax.axis_size("owner")
    slots, heads, key_dim, value_dim = prefix_store.shape
    total = groups * owners
    length = queries.shape[0]
    key_heads = queries.shape[1] // key_dim
    chunks = heads * key_dim // total
    vmem = pl.BlockSpec(memory_space=pltpu.VMEM)
    anywhere = pl.BlockSpec(memory_space=pl.ANY)

    def buffer(rows):
        return pltpu.VMEM((chunks, rows, value_dim), F32)

    out_shape = [
        jax.ShapeDtypeStruct((length, heads * value_dim), BF16),
        jax.ShapeDtypeStruct((chunks, total, value_dim), F32),
    ]
    out_specs = [vmem, vmem]
    scratch = []
    if packed:
        cell = LOW["group"] * LOW["owner"]
        n_y, n_z = groups // LOW["group"], owners // LOW["owner"]
        assert n_y == n_z == 8 and cell == 8 and n_z * 2 * cell == 128
        out_shape.append(jax.ShapeDtypeStruct((1, 1), F32))
        out_specs.append(pl.BlockSpec(memory_space=pltpu.SMEM))
        scratch = [
            pltpu.VMEM((chunks, 2, total, value_dim), F32),
            buffer(2 * total), buffer(2 * total), buffer(n_y * n_z * CELL),
            pltpu.VMEM((2, total, 128), jnp.int32),
            pltpu.VMEM((CELL * n_z, 2 * cell * n_z), BF16),
            pltpu.VMEM((2, PLANE, n_y * CELL), BF16),
        ]
        spread = [n_y * n_z * CELL, n_z * PLANE, n_z * PLANE]
    else:
        spread = [2 * total] * 3
    results = pl.pallas_call(
        functools.partial(kernel, packed, groups, owners, chunks, heads, key_heads, length),
        out_shape=out_shape,
        in_specs=[anywhere] + [vmem] * 7,
        out_specs=out_specs,
        scratch_shapes=scratch + [buffer(rows) for rows in spread] + [buffer(total)] * 11 + [
            pltpu.VMEM((2, total, spread[2]), BF16),
            pltpu.VMEM((2, total, total), BF16),
            pltpu.VMEM((heads, length, 2 * length), BF16),
            pltpu.VMEM((heads, length, 2 * length), BF16),
            pltpu.VMEM((length, heads), F32),
            pltpu.VMEM((heads, length), F32),
            pltpu.VMEM((length, heads), F32),
            pltpu.SemaphoreType.DMA((chunks, 9)),
            pltpu.SemaphoreType.DMA((chunks, 9)),
            pltpu.SemaphoreType.DMA((chunks, 2)),
        ],
        compiler_params=pltpu.CompilerParams(
            collective_id=0 if packed else 1, has_side_effects=True,
            vmem_limit_bytes=56 * 1024 * 1024,
        ),
        cost_estimate=pl.CostEstimate(
            flops=4 * 10**9, bytes_accessed=6 * 2**20, transcendentals=2**19
        ),
    )(
        prefix_store.reshape(slots, chunks, total, value_dim),
        queries, key_rows, values, log_decay.T, write_rate.T,
        hit_state.reshape(1, total), save_slot.reshape(1, total),
    )
    results = list(results)
    results[1] = results[1].reshape(1, heads, key_dim, value_dim)
    return results


def body(*args):
    head_output, checkpoints, excess = run(True, *args)
    return lax.cond(
        excess[0, 0] > 0,
        lambda operands, done: tuple(run(False, *operands)),
        lambda operands, done: done,
        args, (head_output, checkpoints),
    )


def solution(mesh):
    split_rows = P(("group", "owner"), None)
    split_states = P(("group", "owner"), None, None, None)
    in_specs = (split_states,) + (split_rows,) * 5 + (P(), P())
    return jax.shard_map(
        body, mesh=mesh, in_specs=in_specs, out_specs=(split_rows, split_states), check_vma=False
    )
```
